512 devices in a mesh: wide: 64 (over y_hi, z, x), narrow: 8 (over y_lo, core).
Axes of the slice: x: 4, y: 8 (y_hi: 2, y_lo: 4; y = y_hi * 4 + y_lo), z: 8, core: 2. Of those that a mesh axis runs over, the one named last changes fastest.
Arguments:
- x_branch: bfloat16 [8, 4096, 5120], P('narrow', 'wide'), may hold values from -6 to 6
- w_kv: bfloat16 [5120, 1024], P(None, 'narrow'), may hold values from -0.078125 to 0.078125
- k_gain: float32 [512], replicated, may hold values from 0.1 to 1.9
- q_branch: bfloat16 [8, 4096, 2560], P('narrow', 'wide')
- prefix_kv: bfloat16 [8, 1024, 1024], P('narrow', 'wide')
- tree_parent: int32 [8, 64], P('narrow', 'wide'), may hold values from -1 to 3, as said below
Outputs:
- attended: bfloat16 [8, 4096, 2560], P('narrow', 'wide')
The draws below stay inside these ranges and needn't reach their ends.
Inputs may be any that keep to these rules, and one draw needn't show every extreme that they name: `tree_parent`: branches 0 to 3 of every tree have parent -1; every other branch has a parent among them, and every one of them is a parent.
All inputs are finite; a program needn't handle non-finite values.
Results may differ from the reference program's by a relative error of at most 0.012.
Values may be sent and summed in bfloat16 or wider, within the bound.
No kernel may reach another device: no remote copies, remote signals or barrier semaphores. Data moves between devices by JAX's collectives and lax.ppermute only.
A program may use at most 64 MiB of HBM per device.

```python
import jax
import jax.numpy as jnp
from jax import lax

D = 5120
QUERY_HEADS = 20
KEY_VALUE_HEADS = 4
HEAD_SIZE = 128
BRANCH_SLICE = 64
TRUNKS = 4
KEY_WIDTH = 512
QW = 2560
PREFIX = 1024
BRANCHES = 64
BRANCH_TOKENS = 4096
PROMPT_TREES = 8


def shared_prefix(key):
    base = jnp.clip(jax.random.normal(key, (PROMPT_TREES, PREFIX, 2 * KEY_WIDTH), jnp.float32), -6.0, 6.0)
    span_p = PREFIX // 4
    span_q = BRANCH_TOKENS // 4
    tok = jnp.arange(4)[None, :] * span_p + jax.random.randint(jax.random.fold_in(key, 101), (PROMPT_TREES, 4), 0, span_p - 1)
    rows = jnp.arange(4)[None, :] * span_q + jax.random.randint(jax.random.fold_in(key, 102), (PROMPT_TREES, 4), 0, span_q)
    trees = jnp.broadcast_to(jnp.arange(PROMPT_TREES)[:, None], (PROMPT_TREES, 4))
    partner = base[trees, tok + 1]
    new_keys = partner[..., :KEY_WIDTH]
    partner = jnp.concatenate([new_keys, partner[..., KEY_WIDTH:]], axis=-1)
    base = base.at[trees, tok + 1].set(partner)
    return (base, rows, trees)


def draw_prefix_kv(key, part):
    base, rows, trees = shared_prefix(key)
    return base.astype(jnp.bfloat16)


def draw_q_branch(key, part):
    noise = jnp.clip(jax.random.normal(jax.random.fold_in(key, 11), (PROMPT_TREES, BRANCH_TOKENS, QUERY_HEADS * HEAD_SIZE), jnp.float32), -6.0, 6.0)
    base, rows, trees = shared_prefix(key)
    current = noise[trees, rows]
    return noise.at[trees, rows].set(current).astype(jnp.bfloat16)


def draw_tree_parent(key, part):
    key = jax.random.fold_in(key, 5)
    child = jax.random.randint(key, (PROMPT_TREES, BRANCHES - TRUNKS), 0, TRUNKS)
    offset = jax.random.randint(jax.random.fold_in(key, 6), (PROMPT_TREES, 1), 0, TRUNKS)
    first = (jnp.arange(TRUNKS)[None, :] + offset) % TRUNKS
    child = child.at[:, :TRUNKS].set(first)
    roots = -jnp.ones((PROMPT_TREES, TRUNKS), jnp.int32)
    return jnp.concatenate([roots, child.astype(jnp.int32)], axis=1)


def steps_of(stream_key, dims, cuts, smallest, high):
    def one(dim, blocks):
        heights = jax.random.uniform(jax.random.fold_in(jax.random.fold_in(stream_key, 6), dim), (blocks,), jnp.float32, smallest / len(cuts), high / len(cuts))
        return jnp.repeat(jnp.exp(heights), dims[dim] // blocks).reshape((-1,) + (1,) * (len(dims) - dim - 1))

    factor_of = one(*cuts[0])
    for cut in cuts[1:]:
        factor_of = factor_of * one(*cut)
    return factor_of


def normal_values(rng, extent, width, limit, cuts=(), kind=jnp.bfloat16):
    entries = jax.random.normal(rng, extent, jnp.float32) * width
    if len(cuts) > 0:
        entries = steps_of(rng, extent, cuts, -0.22, 0.18) * entries
    return jnp.clip(entries, min=-limit, max=limit).astype(kind)


def setup_inputs(seed: int = 0) -> dict:
    key_list = jax.random.split(jax.random.key(seed), 7)
    x_branch = normal_values(key_list[0], (PROMPT_TREES, BRANCH_TOKENS, D), 1.0, 6.0, ((0, 8), (1, 64)))
    w_kv = normal_values(key_list[1], (D, 2 * KEY_WIDTH), D ** -0.5, 0.078125, ((1, 8),))
    k_gain = jnp.clip(1.0 + 0.18 * jax.random.normal(key_list[2], (KEY_WIDTH,), jnp.float32), 0.1, 1.9)
    q_branch = draw_q_branch(jax.random.fold_in(key_list[6], 71), 0)
    prefix_kv = draw_prefix_kv(jax.random.fold_in(key_list[6], 71), 0)
    tree_parent = draw_tree_parent(jax.random.fold_in(key_list[6], 71), 0)
    return {"x_branch": x_branch, "w_kv": w_kv, "k_gain": k_gain, "q_branch": q_branch, "prefix_kv": prefix_kv, "tree_parent": tree_parent}


neg_big = -1e+30

def rotate_head_rows(key_rows, token_positions):
    half = HEAD_SIZE // 2
    index = jnp.arange(half, dtype=jnp.float32)
    inverse = jnp.exp(-jnp.log(jnp.float32(500000.0)) * 2.0 * index / HEAD_SIZE)
    angle = token_positions.astype(jnp.float32)[:, None, None] * inverse[None, None, :]
    cosine = jnp.cos(angle)
    sine = jnp.sin(angle)
    first = key_rows[..., :half]
    second = key_rows[..., half:]
    return jnp.concatenate([first * cosine - second * sine, second * cosine + first * sine], axis=-1)

def tree_keys(x_tree, w_kv, k_gain, parents):
    kv = jnp.dot(x_tree, w_kv, preferred_element_type=jnp.float32)
    key_rows = kv[:, :KEY_WIDTH]
    meansq = lax.optimization_barrier(jnp.mean(key_rows * key_rows, axis=-1, keepdims=True))
    key_rows = key_rows * lax.rsqrt(meansq + 1e-06) * k_gain
    child = (parents >= 0).astype(jnp.int32)
    inside = jnp.arange(BRANCH_SLICE, dtype=jnp.int32)
    token_positions = (PREFIX + inside[None, :] + BRANCH_SLICE * child[:, None]).reshape(BRANCH_TOKENS)
    key_rows = rotate_head_rows(key_rows.reshape(BRANCH_TOKENS, KEY_VALUE_HEADS, HEAD_SIZE), token_positions).reshape(BRANCH_TOKENS, KEY_WIDTH)
    return jnp.concatenate([key_rows.astype(jnp.bfloat16), kv[:, KEY_WIDTH:].astype(jnp.bfloat16)], axis=1)

def one_tree(items, w_kv, k_gain):
    x_tree, q_tree, prefix_tree, parents = items
    own_kv = tree_keys(x_tree, w_kv, k_gain, parents)
    query_group = QUERY_HEADS // KEY_VALUE_HEADS
    inside = jnp.arange(BRANCH_SLICE, dtype=jnp.int32)
    causal = jnp.where(inside[None, :] <= inside[:, None], 0.0, neg_big).astype(jnp.float32)

    def one_branch(branch):
        parent = parents[branch]
        start = (branch * BRANCH_SLICE).astype(jnp.int32)
        pstart = (jnp.maximum(parent, 0) * BRANCH_SLICE).astype(jnp.int32)
        own = lax.dynamic_slice_in_dim(own_kv, start, BRANCH_SLICE, 0)
        above = lax.dynamic_slice_in_dim(own_kv, pstart, BRANCH_SLICE, 0)
        query_matrix = lax.dynamic_slice_in_dim(q_tree, start, BRANCH_SLICE, 0)
        joined_key_value = jnp.concatenate([prefix_tree, above, own], axis=0)
        token_count = joined_key_value.shape[0]
        parent_mask = jnp.where(parent >= 0, 0.0, neg_big).astype(jnp.float32) * jnp.ones((BRANCH_SLICE, BRANCH_SLICE), jnp.float32)
        mask = jnp.concatenate([jnp.zeros((BRANCH_SLICE, PREFIX), jnp.float32), parent_mask, causal], axis=1)
        key_rows = joined_key_value[:, :KEY_WIDTH].reshape(token_count, KEY_VALUE_HEADS, HEAD_SIZE).astype(jnp.float32)
        value_rows = joined_key_value[:, KEY_WIDTH:].reshape(token_count, KEY_VALUE_HEADS, HEAD_SIZE).astype(jnp.float32)
        query_four = query_matrix.reshape(BRANCH_SLICE, KEY_VALUE_HEADS, query_group, HEAD_SIZE).astype(jnp.float32)
        score = jnp.einsum('rgjd,ngd->rgjn', query_four, key_rows) * HEAD_SIZE ** (-0.5) + mask[:, None, None, :]
        top = lax.optimization_barrier(jnp.max(score, axis=-1, keepdims=True))
        expo = jnp.exp(score - top)
        total = lax.optimization_barrier(jnp.sum(expo, axis=-1))
        weight = expo.astype(jnp.bfloat16).astype(jnp.float32)
        summed = jnp.einsum('rgjn,ngd->rgjd', weight, value_rows)
        return (summed / total[..., None]).reshape(BRANCH_SLICE, QW).astype(jnp.bfloat16)
    outputs = lax.map(one_branch, jnp.arange(BRANCHES, dtype=jnp.int32))
    return outputs.reshape(BRANCH_TOKENS, QW)

def reference(x_branch, w_kv, k_gain, q_branch, prefix_kv, tree_parent):
    return lax.map(lambda items: one_tree(items, w_kv, k_gain), (x_branch, q_branch, prefix_kv, tree_parent))
```

```python
import functools
import math

import jax
import jax.numpy as jnp
from jax import lax
from jax.experimental import pallas as pl
from jax.experimental.pallas import tpu as pltpu
from jax.sharding import PartitionSpec as P

HEAD = 128
HEADS_KV = 4
GROUP = 5
ROWS = 64
KEY_WIDTH = 512
PREFIX = 1024
SCALE = HEAD ** -0.5 * math.log2(math.e)
NEG = -1e30

FLAT = ("wide", "narrow")


def index_of(y, z, x, c):
    return ((((y // 4) * 8 + z) * 4 + x) * 4 + y % 4) * 2 + c


def move(value, target, only=None):
    pairs = []
    for y in range(8):
        for z in range(8):
            for x in range(4):
                for c in range(2):
                    if only is None or only(y, z, x, c):
                        ty, tz, tx, tc = target(y, z, x, c)
                        pairs.append(
                            (index_of(y, z, x, c), index_of(ty % 8, tz % 8, tx % 4, tc % 2))
                        )
    return lax.ppermute(value, FLAT, pairs)


def along_y(value, s):
    return move(value, lambda y, z, x, c: (y + s, z, x, c))


def along_x(value, s):
    return move(value, lambda y, z, x, c: (y, z, x + s, c))


VM = pl.BlockSpec(memory_space=pltpu.VMEM)
SM = pl.BlockSpec(memory_space=pltpu.SMEM)
PARAMS = pltpu.CompilerParams(vmem_limit_bytes=40 * 1024 * 1024)


def cost(flops, moved, trans=0):
    return pl.CostEstimate(flops=flops, bytes_accessed=moved, transcendentals=trans)


def project_kernel(n, where_ref, *refs):
    rows, (own_ref, other_ref), outs = refs[:n], refs[n : n + 2], refs[n + 2 :]
    core = where_ref[0]
    for row, out in zip(rows, outs):
        for side, w in ((core, own_ref), (1 - core, other_ref)):
            got = jnp.dot(row[...], w[...], preferred_element_type=jnp.float32)
            out[:, pl.ds(pl.multiple_of(side * 128, 128), 128)] = got.astype(jnp.bfloat16)


def project(where, rows, w_own, w_other):
    n = len(rows)
    total = sum(r.shape[0] for r in rows)
    return pl.pallas_call(
        functools.partial(project_kernel, n),
        out_shape=[jax.ShapeDtypeStruct((r.shape[0], 256), jnp.bfloat16) for r in rows],
        in_specs=[SM] + [VM] * (n + 2),
        out_specs=[VM] * n,
        compiler_params=PARAMS,
        cost_estimate=cost(2 * total * 5120 * 256, 5120 * 512 + total * 10240),
    )(where, *rows, w_own, w_other)


def finish_kernel(where_ref, p0, p1, p2a, p2b, p3, gain_ref, cos_ref, sin_ref, out_ref):
    yl = where_ref[1]
    pieces = [
        p0[...].astype(jnp.float32),
        p1[...].astype(jnp.float32),
        jnp.concatenate([p2a[...], p2b[...]], axis=0).astype(jnp.float32),
        p3[...].astype(jnp.float32),
    ]

    def piece(j):
        d = (j - yl) & 3
        return jnp.where(
            d == 0, pieces[0], jnp.where(d == 1, pieces[1], jnp.where(d == 2, pieces[2], pieces[3]))
        )

    keys = jnp.concatenate([piece(0), piece(1)], axis=1)
    meansq = jnp.mean(keys * keys, axis=-1, keepdims=True)
    keys = keys * lax.rsqrt(meansq + 1e-06) * gain_ref[...]
    cosine, sine = cos_ref[...], sin_ref[...]
    for h in range(HEADS_KV):
        k = keys[:, h * HEAD : (h + 1) * HEAD]
        out_ref[:, h * HEAD : (h + 1) * HEAD] = (
            k * cosine + pltpu.roll(k, 64, 1) * sine
        ).astype(jnp.bfloat16)
    out_ref[:, 512:768] = piece(2).astype(jnp.bfloat16)
    out_ref[:, 768:1024] = piece(3).astype(jnp.bfloat16)


def finish(where, pieces, gain, cosine, sine):
    return pl.pallas_call(
        finish_kernel,
        out_shape=jax.ShapeDtypeStruct((ROWS, 1024), jnp.bfloat16),
        in_specs=[SM] + [VM] * 8,
        out_specs=VM,
        compiler_params=PARAMS,
        cost_estimate=cost(64 * 512 * 10, 600000),
    )(where, *pieces, gain, cosine, sine)


def queries(q_ref, g):
    first = g * GROUP
    return jnp.concatenate(
        [q_ref[:, (first + j) * HEAD : (first + j + 1) * HEAD] for j in range(GROUP)], axis=0
    )


def scores(q, k):
    return lax.dot_general(
        q, k, (((1,), (1,)), ((), ())), preferred_element_type=jnp.float32
    ) * SCALE


def prefix_kernel(n, q_ref, *refs):
    blocks, (high_ref, total_ref, sum_ref) = refs[:n], refs[n:]
    for g in range(HEADS_KV):
        q = queries(q_ref, g)
        high = total = acc = None
        for block in blocks:
            s = scores(q, block[:, g * HEAD : (g + 1) * HEAD])
            v = block[:, KEY_WIDTH + g * HEAD : KEY_WIDTH + (g + 1) * HEAD]
            top = jnp.max(s, axis=-1, keepdims=True)
            new = top if high is None else jnp.maximum(high, top)
            p = jnp.exp2(s - new)
            part = jnp.sum(p, axis=-1, keepdims=True)
            pv = jnp.dot(p.astype(jnp.bfloat16), v, preferred_element_type=jnp.float32)
            if high is None:
                total, acc = part, pv
            else:
                factor = jnp.exp2(high - new)
                total, acc = total * factor + part, acc * factor + pv
            high = new
        high_ref[g] = high
        total_ref[g] = total
        sum_ref[g] = acc


def prefix_attend(q, blocks):
    n = len(blocks)
    m = ROWS * GROUP
    keys = sum(b.shape[0] for b in blocks)
    return pl.pallas_call(
        functools.partial(prefix_kernel, n),
        out_shape=[
            jax.ShapeDtypeStruct((HEADS_KV, m, 1), jnp.float32),
            jax.ShapeDtypeStruct((HEADS_KV, m, 1), jnp.float32),
            jax.ShapeDtypeStruct((HEADS_KV, m, HEAD), jnp.float32),
        ],
        in_specs=[VM] * (n + 1),
        out_specs=[VM] * 3,
        compiler_params=PARAMS,
        cost_estimate=cost(4 * 1280 * keys * 128, keys * 2048 + 2000000, 1280 * keys),
    )(q, *blocks)


def last_kernel(where_ref, q_ref, t0, t1, t2, t3, own_ref, high_ref, total_ref, sum_ref, out_ref):
    x, parent = where_ref[2], where_ref[3]
    child = parent >= 0
    d = (parent - x) & 3
    row = lax.broadcasted_iota(jnp.int32, (ROWS, 2 * ROWS), 0)
    col = lax.broadcasted_iota(jnp.int32, (ROWS, 2 * ROWS), 1)
    use = (jnp.where(child, 1, 0) * jnp.where(col < ROWS, 1, 0)) + jnp.where(
        (col >= ROWS) & (col - ROWS <= row), 1, 0
    )
    use = jnp.concatenate([use] * GROUP, axis=0) > 0

    def pick(lo):
        a, b, c, e = (t[:, lo : lo + HEAD].astype(jnp.float32) for t in (t0, t1, t2, t3))
        return jnp.where(d == 0, a, jnp.where(d == 1, b, jnp.where(d == 2, c, e))).astype(
            jnp.bfloat16
        )

    for g in range(HEADS_KV):
        q = queries(q_ref, g)
        lo, hi = g * HEAD, KEY_WIDTH + g * HEAD
        k = jnp.concatenate([pick(lo), own_ref[:, lo : lo + HEAD]], axis=0)
        v = jnp.concatenate([pick(hi), own_ref[:, hi : hi + HEAD]], axis=0)
        s = jnp.where(use, scores(q, k), NEG)
        high = high_ref[g]
        new = jnp.maximum(high, jnp.max(s, axis=-1, keepdims=True))
        p = jnp.exp2(s - new)
        factor = jnp.exp2(high - new)
        total = total_ref[g] * factor + jnp.sum(p, axis=-1, keepdims=True)
        acc = sum_ref[g] * factor + jnp.dot(
            p.astype(jnp.bfloat16), v, preferred_element_type=jnp.float32
        )
        acc = (acc / total).astype(jnp.bfloat16)
        for j in range(GROUP):
            lo = (g * GROUP + j) * HEAD
            out_ref[:, lo : lo + HEAD] = acc[j * ROWS : (j + 1) * ROWS]


def last_attend(where, q, trunks, own, state):
    return pl.pallas_call(
        last_kernel,
        out_shape=jax.ShapeDtypeStruct((ROWS, HEADS_KV * GROUP * HEAD), jnp.bfloat16),
        in_specs=[SM] + [VM] * 9,
        out_specs=VM,
        compiler_params=PARAMS,
        cost_estimate=cost(4 * 1280 * 128 * 128, 3000000, 1280 * 128),
    )(where, q, *trunks, own, *state)


def local(x_branch, w_kv, k_gain, q_branch, prefix_kv, tree_parent):
    wide, narrow = lax.axis_index("wide"), lax.axis_index("narrow")
    yh, z, x = wide // 32, (wide // 4) % 8, wide % 4
    yl, core = narrow // 2, narrow % 2
    parent = tree_parent[0, 0]
    where = jnp.stack([core, yl, x, parent]).astype(jnp.int32)

    rows = x_branch[0]
    half = ROWS // 2
    w_other = move(w_kv, lambda y, z, x, c: (y, z, x, 1 - c))
    below = along_y(rows, 1)
    above = along_y(rows, -1)
    below2 = along_y(below[:half], 1)
    above2 = along_y(above[half:], -1)

    piece = prefix_kv[0]
    piece = jnp.concatenate([piece, along_y(piece, 4)], axis=0)
    for bit in (4, 2, 1):
        got = move(piece, lambda y, z, x, c: (y, z ^ bit, x, c))
        piece = jnp.concatenate([piece, got], axis=0)
    quarter = piece.shape[0] // 2
    left = along_x(piece, 1)
    right = along_x(piece, -1)
    left2 = along_x(left[:quarter], 1)
    right2 = along_x(right[quarter:], -1)
    state = prefix_attend(q_branch[0], [piece, left, right, left2, right2])

    mine, for_below, for_above = project(where, [rows, below, above], w_kv, w_other)
    for_below2, for_above2 = project(where, [below2, above2], w_kv, w_other)
    from_above = along_y(for_below, -1)
    from_below = along_y(for_above, 1)
    from_above2 = along_y(for_below2, -2)
    from_below2 = along_y(for_above2, 2)

    index = jnp.arange(64, dtype=jnp.float32)
    inverse = jnp.exp(-jnp.log(jnp.float32(500000.0)) * 2.0 * index / HEAD)
    inside = jnp.arange(ROWS, dtype=jnp.int32)
    positions = PREFIX + inside + ROWS * (parent >= 0).astype(jnp.int32)
    angle = positions.astype(jnp.float32)[:, None] * inverse[None, :]
    cosine, sine = jnp.cos(angle), jnp.sin(angle)
    cosine = jnp.concatenate([cosine, cosine], axis=1)
    sine = jnp.concatenate([-sine, sine], axis=1)
    own = finish(
        where,
        [mine, from_above, from_above2, from_below2, from_below],
        k_gain[None, :],
        cosine,
        sine,
    )

    root = (yh == 0) & (z == 0)
    first = lambda y, z, x, c: y < 4 and z == 0
    have = jnp.where(root, own, jnp.zeros_like(own))
    have = (
        have
        + move(own, lambda y, z, x, c: (y, 4, x, c), first)
        + move(own, lambda y, z, x, c: (y + 4, 0, x, c), first)
        + move(own, lambda y, z, x, c: (y + 4, 4, x, c), first)
    )
    second = lambda y, z, x, c: z % 4 == 0
    trunk = (
        have
        + move(have, lambda y, z, x, c: (y, z + 1, x, c), second)
        + move(have, lambda y, z, x, c: (y, z - 1, x, c), second)
        + move(have, lambda y, z, x, c: (y, z + 2, x, c), second)
    )
    trunks = [trunk, along_x(trunk, -1), along_x(trunk, 2), along_x(trunk, 1)]
    return last_attend(where, q_branch[0], trunks, own, state)[None]


def solution(mesh):
    placed = (
        P("narrow", "wide", None),
        P(None, "narrow"),
        P(),
        P("narrow", "wide", None),
        P("narrow", "wide", None),
        P("narrow", "wide"),
    )
    return jax.shard_map(
        local, mesh=mesh, in_specs=placed, out_specs=P("narrow", "wide", None), check_vma=False
    )
```

```python
import functools
import math

import jax
import jax.numpy as jnp
from jax import lax
from jax.experimental import pallas as pl
from jax.experimental.pallas import tpu as pltpu
from jax.sharding import PartitionSpec as P

HEAD = 128
HEADS_KV = 4
GROUP = 5
ROWS = 64
KEY_WIDTH = 512
PREFIX = 1024
SCALE = HEAD ** -0.5 * math.log2(math.e)
NEG = -1e30

PARTS = ("yh", "z", "x", "yl", "core")
SIZES = (2, 8, 4, 4, 2)
WIDE, NARROW = PARTS[:3], PARTS[3:]
Y = ("yh", "yl")


NEXT_A = [(i, i ^ 1) for i in range(8)]
NEXT_B = [(i, (i + (1 if i % 2 else -1)) % 8) for i in range(8)]


X_NEXT_A = [(i, i ^ 1) for i in range(4)]
X_NEXT_B = [(i, 3 - i) for i in range(4)]


def ring_x(value, pairs):
    return lax.ppermute(value, "x", pairs)


def along_x(value, s):
    return lax.ppermute(value, "x", [(i, (i + s) % 4) for i in range(4)])


def along_y(value, pairs):
    return lax.ppermute(value, Y, pairs)


def along_z(value, bit):
    return lax.ppermute(value, "z", [(i, i ^ bit) for i in range(8)])


def swap(value):
    return lax.ppermute(value, "core", [(0, 1), (1, 0)])


def along_yh_z(value, pairs):
    return lax.ppermute(value, ("yh", "z"), [(a * 8 + b, c * 8 + d) for a, b, c, d in pairs])


VM = pl.BlockSpec(memory_space=pltpu.VMEM)
SM = pl.BlockSpec(memory_space=pltpu.SMEM)
PARAMS = pltpu.CompilerParams(vmem_limit_bytes=40 * 1024 * 1024)


def cost(flops, moved, trans=0):
    return pl.CostEstimate(flops=flops, bytes_accessed=moved, transcendentals=trans)


ANY = pl.BlockSpec(memory_space=pl.ANY)
DEPTH = 5120
HALF = DEPTH // 2


def join_kernel(n, *refs):
    parts, out_ref = refs[:n], refs[-1]
    at = 0
    for part in parts:
        out_ref[at : at + part.shape[0]] = part[...]
        at += part.shape[0]


def join(parts, after=()):
    n = len(parts)
    total = sum(p.shape[0] for p in parts)
    width = parts[0].shape[1]
    return pl.pallas_call(
        functools.partial(join_kernel, n),
        out_shape=jax.ShapeDtypeStruct((total, width), parts[0].dtype),
        in_specs=[VM] * n + [ANY] * len(after),
        out_specs=VM,
        compiler_params=PARAMS,
        cost_estimate=cost(0, 4 * total * width),
    )(*parts, *after)


def pack_kernel(rows_ref, w_ref, after_ref, for_a_ref, for_b_ref):
    for_b_ref[:HALF] = w_ref[:HALF]
    for_a_ref[:HALF] = w_ref[HALF:]
    for i in range(HALF // 128):
        at = HALF + i * ROWS
        for_a_ref[at : at + ROWS] = rows_ref[:, i * 128 : (i + 1) * 128]
        for_b_ref[at : at + ROWS] = rows_ref[:, HALF + i * 128 : HALF + (i + 1) * 128]


def pack(rows, w, after):
    out = jax.ShapeDtypeStruct((HALF + HALF // 128 * ROWS, 128), rows.dtype)
    return pl.pallas_call(
        pack_kernel,
        out_shape=[out, out],
        in_specs=[VM, VM, ANY],
        out_specs=[VM] * 2,
        compiler_params=PARAMS,
        cost_estimate=cost(0, 4 * (rows.size + w.size)),
    )(rows, w, after)


def weights_kernel(from_a_ref, from_b_ref, piece_ref, q_ref, out_ref):
    out_ref[:HALF] = from_b_ref[:HALF]
    out_ref[HALF:] = from_a_ref[:HALF]


def weights(from_a, from_b, *after):
    return pl.pallas_call(
        weights_kernel,
        out_shape=jax.ShapeDtypeStruct((DEPTH, 128), from_a.dtype),
        in_specs=[VM, VM, ANY, ANY],
        out_specs=VM,
        compiler_params=PARAMS,
        cost_estimate=cost(0, 4 * DEPTH * 128),
    )(from_a, from_b, *after)


def project_kernel(
    where_ref, rows, own, other, from_a, from_b, came_other, local_ref, to_a_ref, to_b_ref
):
    first = where_ref[0] == 0

    def product(at, far, near):
        acc = None
        for k in range(0, HALF, 512):
            blocks = [HALF + (k // 128 + i) * ROWS for i in range(4)]
            x = jnp.concatenate([far[b : b + ROWS] for b in blocks], axis=1)
            x = jnp.concatenate([rows[:, at + k : at + k + 512], x], axis=0)
            w = jnp.concatenate(
                [
                    own[at + k : at + k + 512],
                    other[at + k : at + k + 512],
                    near[k : k + 512],
                    came_other[at + k : at + k + 512],
                ],
                axis=1,
            )
            got = jnp.dot(x, w, preferred_element_type=jnp.float32)
            acc = got if acc is None else acc + got
        a, b, c, d = (acc[:, i * 128 : (i + 1) * 128] for i in range(4))
        return jnp.concatenate(
            [
                jnp.where(first, a, b),
                jnp.where(first, b, a),
                jnp.where(first, c, d),
                jnp.where(first, d, c),
            ],
            axis=1,
        )

    one = product(0, from_a, from_b)
    two = product(HALF, from_b, from_a)
    local_ref[:, :256] = one[:ROWS, :256] + two[:ROWS, :256]
    local_ref[:, 256:512] = two[:ROWS, 256:]
    local_ref[:, 512:] = one[:ROWS, 256:]
    to_a_ref[...] = one[ROWS:].astype(jnp.bfloat16)
    to_b_ref[...] = two[ROWS:].astype(jnp.bfloat16)


def project(where, *arrays):
    back = jax.ShapeDtypeStruct((ROWS, 512), jnp.bfloat16)
    return pl.pallas_call(
        project_kernel,
        out_shape=[jax.ShapeDtypeStruct((ROWS, 768), jnp.float32), back, back],
        in_specs=[SM] + [VM] * 6,
        out_specs=[VM] * 3,
        compiler_params=PARAMS,
        cost_estimate=cost(4 * 2 * ROWS * HALF * 512, 7000000),
    )(where, *arrays)


def finish_kernel(where_ref, local_ref, got_a, got_b, gain_ref, cos_ref, sin_ref, out_ref, piece_ref):
    y = where_ref[1]
    even = (y & 1) == 0
    a = got_a[:, :256].astype(jnp.float32) + local_ref[:, 256:512]
    b = got_b[:, :256].astype(jnp.float32) + local_ref[:, 512:]
    piece_ref[0] = local_ref[:, :256]
    piece_ref[1] = jnp.where(even, a, b)
    piece_ref[2] = got_a[:, 256:].astype(jnp.float32) + got_b[:, 256:].astype(jnp.float32)
    piece_ref[3] = jnp.where(even, b, a)
    a, b, c, d = (piece_ref[(j - y) & 3] for j in range(4))
    keys = jnp.concatenate([a, b], axis=1)
    meansq = jnp.mean(keys * keys, axis=-1, keepdims=True)
    keys = keys * lax.rsqrt(meansq + 1e-06) * gain_ref[...]
    cosine, sine = cos_ref[...], sin_ref[...]
    for h in range(HEADS_KV):
        k = keys[:, h * HEAD : (h + 1) * HEAD]
        out_ref[:, h * HEAD : (h + 1) * HEAD] = (
            k * cosine + pltpu.roll(k, 64, 1) * sine
        ).astype(jnp.bfloat16)
    out_ref[:, 512:768] = c.astype(jnp.bfloat16)
    out_ref[:, 768:1024] = d.astype(jnp.bfloat16)


def finish(where, here, got_a, got_b, gain, cosine, sine):
    return pl.pallas_call(
        finish_kernel,
        out_shape=jax.ShapeDtypeStruct((ROWS, 1024), jnp.bfloat16),
        in_specs=[SM] + [VM] * 6,
        out_specs=VM,
        scratch_shapes=[pltpu.VMEM((4, ROWS, 256), jnp.float32)],
        compiler_params=PARAMS,
        cost_estimate=cost(64 * 512 * 10, 600000),
    )(where, here, got_a, got_b, gain, cosine, sine)


def queries(q_ref, g):
    first = g * GROUP
    return jnp.concatenate(
        [q_ref[:, (first + j) * HEAD : (first + j + 1) * HEAD] for j in range(GROUP)], axis=0
    )


def scores(q, k):
    return lax.dot_general(
        q, k, (((1,), (1,)), ((), ())), preferred_element_type=jnp.float32
    ) * SCALE


def prefix_kernel(n, q_ref, q2_ref, *refs):
    blocks, (high_ref, total_ref, sum_ref, send_ref) = refs[:n], refs[-4:]
    lane = lax.broadcasted_iota(jnp.int32, (ROWS, HEAD), 1)
    logs = jnp.zeros((ROWS, HEAD), jnp.float32)

    def attend(q, g):
        high = total = acc = None
        for block in blocks:
            s = scores(q, block[:, g * HEAD : (g + 1) * HEAD])
            v = block[:, KEY_WIDTH + g * HEAD : KEY_WIDTH + (g + 1) * HEAD]
            top = jnp.max(s, axis=-1, keepdims=True)
            new = top if high is None else jnp.maximum(high, top)
            p = jnp.exp2(s - new)
            part = jnp.sum(p, axis=-1, keepdims=True)
            pv = jnp.dot(p.astype(jnp.bfloat16), v, preferred_element_type=jnp.float32)
            if high is None:
                total, acc = part, pv
            else:
                factor = jnp.exp2(high - new)
                total, acc = total * factor + part, acc * factor + pv
            high = new
        return high, total, acc

    for g in range(HEADS_KV):
        high, total, acc = attend(queries(q2_ref, g), g)
        acc = (acc / total).astype(jnp.bfloat16)
        log = high + jnp.log2(total)
        for j in range(GROUP):
            h = g * GROUP + j
            send_ref[:, h * HEAD : (h + 1) * HEAD] = acc[j * ROWS : (j + 1) * ROWS]
            logs = jnp.where(lane == h, log[j * ROWS : (j + 1) * ROWS], logs)
        high_ref[g], total_ref[g], sum_ref[g] = attend(queries(q_ref, g), g)
    for part in range(3):
        at = (20 + part) * HEAD
        piece = logs.astype(jnp.bfloat16)
        send_ref[:, at : at + HEAD] = piece
        logs = logs - piece.astype(jnp.float32)


def prefix_attend(q, q2, blocks, after):
    n = len(blocks)
    m = ROWS * GROUP
    keys = 2 * sum(b.shape[0] for b in blocks)
    return pl.pallas_call(
        functools.partial(prefix_kernel, n),
        out_shape=[
            jax.ShapeDtypeStruct((HEADS_KV, m, 1), jnp.float32),
            jax.ShapeDtypeStruct((HEADS_KV, m, 1), jnp.float32),
            jax.ShapeDtypeStruct((HEADS_KV, m, HEAD), jnp.float32),
            jax.ShapeDtypeStruct((ROWS, 23 * HEAD), jnp.bfloat16),
        ],
        in_specs=[VM] * (n + 2) + [ANY] * len(after),
        out_specs=[VM] * 4,
        compiler_params=PARAMS,
        cost_estimate=cost(4 * 1280 * keys * 128, keys * 2048 + 2000000, 1280 * keys),
    )(q, q2, *blocks, *after)


def last_kernel(
    where_ref, q_ref, t0, t1, t2, t3, own_ref, high_ref, total_ref, sum_ref, got_ref, out_ref
):
    x, parent = where_ref[2], where_ref[3]
    child = parent >= 0
    d = (parent - x) & 3
    row = lax.broadcasted_iota(jnp.int32, (ROWS, 2 * ROWS), 0)
    col = lax.broadcasted_iota(jnp.int32, (ROWS, 2 * ROWS), 1)
    use = (jnp.where(child, 1, 0) * jnp.where(col < ROWS, 1, 0)) + jnp.where(
        (col >= ROWS) & (col - ROWS <= row), 1, 0
    )
    use = jnp.concatenate([use] * GROUP, axis=0) > 0

    def pick(lo):
        a, b, c, e = (t[:, lo : lo + HEAD].astype(jnp.float32) for t in (t0, t1, t2, t3))
        return jnp.where(d == 0, a, jnp.where(d == 1, b, jnp.where(d == 2, c, e))).astype(
            jnp.bfloat16
        )

    logs = [got_ref[:, (20 + i) * HEAD : (21 + i) * HEAD].astype(jnp.float32) for i in range(3)]
    logs = logs[0] + logs[1] + logs[2]
    for g in range(HEADS_KV):
        q = queries(q_ref, g)
        lo, hi = g * HEAD, KEY_WIDTH + g * HEAD
        k = jnp.concatenate([pick(lo), own_ref[:, lo : lo + HEAD]], axis=0)
        v = jnp.concatenate([pick(hi), own_ref[:, hi : hi + HEAD]], axis=0)
        s = jnp.where(use, scores(q, k), NEG)
        heads = range(g * GROUP, (g + 1) * GROUP)
        high = high_ref[g]
        log = jnp.concatenate([logs[:, h : h + 1] for h in heads], axis=0)
        result = jnp.concatenate([got_ref[:, h * HEAD : (h + 1) * HEAD] for h in heads], axis=0)
        new = jnp.maximum(jnp.maximum(high, log), jnp.max(s, axis=-1, keepdims=True))
        p = jnp.exp2(s - new)
        factor, factor2 = jnp.exp2(high - new), jnp.exp2(log - new)
        total = total_ref[g] * factor + factor2 + jnp.sum(p, axis=-1, keepdims=True)
        acc = sum_ref[g] * factor + result.astype(jnp.float32) * factor2
        acc = acc + jnp.dot(p.astype(jnp.bfloat16), v, preferred_element_type=jnp.float32)
        acc = (acc / total).astype(jnp.bfloat16)
        for j in range(GROUP):
            lo = (g * GROUP + j) * HEAD
            out_ref[:, lo : lo + HEAD] = acc[j * ROWS : (j + 1) * ROWS]


def last_attend(where, q, trunks, own, state, got):
    return pl.pallas_call(
        last_kernel,
        out_shape=jax.ShapeDtypeStruct((ROWS, HEADS_KV * GROUP * HEAD), jnp.bfloat16),
        in_specs=[SM] + [VM] * 10,
        out_specs=VM,
        compiler_params=PARAMS,
        cost_estimate=cost(4 * 1280 * 128 * 128, 3000000, 1280 * 128),
    )(where, q, *trunks, own, *state, got)


def local(x_branch, w_kv, k_gain, q_branch, prefix_kv, tree_parent):
    y, core = lax.axis_index(Y), lax.axis_index("core")
    parent = tree_parent[0, 0]
    where = jnp.stack([core, y, lax.axis_index("x"), parent]).astype(jnp.int32)

    piece = prefix_kv[0]
    facing = along_y(piece, [(i, (i + 4) % 8) for i in range(8)])

    rows = x_branch[0]
    for_a, for_b = pack(rows, w_kv, facing)
    from_a = along_y(for_a, NEXT_A)
    from_b = along_y(for_b, NEXT_B)
    w_other = swap(w_kv)

    q = q_branch[0]
    q2 = ring_x(q, X_NEXT_A)

    piece = join([piece, facing])
    piece = join([piece, along_z(piece, 4)])
    piece = join([piece, along_z(piece, 2)])
    far = along_z(piece, 1)
    came_other = swap(weights(from_a, from_b, piece, q2))
    here, to_a, to_b = project(where, rows, w_kv, w_other, from_a, from_b, came_other)
    got_a = along_y(to_a, NEXT_A)
    got_b = along_y(to_b, NEXT_B)
    piece = join([piece, far], [to_a])
    beside = ring_x(piece, X_NEXT_B)

    index = jnp.arange(64, dtype=jnp.float32)
    inverse = jnp.exp(-jnp.log(jnp.float32(500000.0)) * 2.0 * index / HEAD)
    inside = jnp.arange(ROWS, dtype=jnp.int32)
    positions = PREFIX + inside + ROWS * (parent >= 0).astype(jnp.int32)
    angle = positions.astype(jnp.float32)[:, None] * inverse[None, :]
    cosine, sine = jnp.cos(angle), jnp.sin(angle)
    cosine = jnp.concatenate([cosine, cosine], axis=1)
    sine = jnp.concatenate([-sine, sine], axis=1)
    own = finish(where, here, got_a, got_b, k_gain[None, :], cosine, sine)

    root = (lax.axis_index("yh") == 0) & (lax.axis_index("z") == 0)
    have = jnp.where(root, own, jnp.zeros_like(own))
    for far in ((0, 4), (1, 0), (1, 4)):
        have = have + along_yh_z(own, [(0, 0) + far])
    trunk = have
    for step in (1, -1, 2):
        trunk = trunk + along_yh_z(
            have, [(a, b, a, (b + step) % 8) for a in range(2) for b in (0, 4)]
        )
    *state, partial = prefix_attend(q, q2, [piece, beside], [have])
    trunks = [trunk, along_x(trunk, -1), along_x(trunk, 2), along_x(trunk, 1)]
    return last_attend(where, q, trunks, own, state, ring_x(partial, X_NEXT_A))[None]


def solution(mesh):
    parts = jax.sharding.Mesh(mesh.devices.reshape(SIZES), PARTS)
    tokens = P(NARROW, WIDE, None)
    placed = (tokens, P(None, NARROW), P(), tokens, tokens, P(NARROW, WIDE))
    return jax.shard_map(local, mesh=parts, in_specs=placed, out_specs=tokens, check_vma=False)
```

```python
import functools
import math

import jax
import jax.numpy as jnp
from jax import lax
from jax.experimental import pallas as pl
from jax.experimental.pallas import tpu as pltpu
from jax.sharding import PartitionSpec as P

HEAD = 128
HEADS_KV = 4
GROUP = 5
ROWS = 64
KEY_WIDTH = 512
PREFIX = 1024
SCALE = HEAD ** -0.5 * math.log2(math.e)
NEG = -1e30

PARTS = ("yh", "z", "x", "yl", "core")
SIZES = (2, 8, 4, 4, 2)
WIDE, NARROW = PARTS[:3], PARTS[3:]
Y = ("yh", "yl")


NEXT_A = [(i, i ^ 1) for i in range(8)]
NEXT_B = [(i, (i + (1 if i % 2 else -1)) % 8) for i in range(8)]


X_NEXT_A = [(i, i ^ 1) for i in range(4)]
X_NEXT_B = [(i, 3 - i) for i in range(4)]


def ring_x(value, pairs):
    return lax.ppermute(value, "x", pairs)


def along_x(value, s):
    return lax.ppermute(value, "x", [(i, (i + s) % 4) for i in range(4)])


def along_y(value, pairs):
    return lax.ppermute(value, Y, pairs)


def along_z(value, bit):
    return lax.ppermute(value, "z", [(i, i ^ bit) for i in range(8)])


def swap(value):
    return lax.ppermute(value, "core", [(0, 1), (1, 0)])


def along_yh_z(value, pairs):
    return lax.ppermute(value, ("yh", "z"), [(a * 8 + b, c * 8 + d) for a, b, c, d in pairs])


VM = pl.BlockSpec(memory_space=pltpu.VMEM)
SM = pl.BlockSpec(memory_space=pltpu.SMEM)
PARAMS = pltpu.CompilerParams(vmem_limit_bytes=20 * 1024 * 1024)


def cost(flops, moved, trans=0):
    return pl.CostEstimate(flops=flops, bytes_accessed=moved, transcendentals=trans)


ANY = pl.BlockSpec(memory_space=pl.ANY)
DEPTH = 5120
HALF = DEPTH // 2


def join_kernel(n, *refs):
    parts, out_ref = refs[:n], refs[-1]
    at = 0
    for part in parts:
        out_ref[at : at + part.shape[0]] = part[...]
        at += part.shape[0]


def join(parts, after=()):
    n = len(parts)
    total = sum(p.shape[0] for p in parts)
    width = parts[0].shape[1]
    return pl.pallas_call(
        functools.partial(join_kernel, n),
        out_shape=jax.ShapeDtypeStruct((total, width), parts[0].dtype),
        in_specs=[VM] * n + [ANY] * len(after),
        out_specs=VM,
        compiler_params=PARAMS,
        cost_estimate=cost(0, 4 * total * width),
    )(*parts, *after)


def pack_kernel(rows_ref, w_ref, after_ref, for_a_ref, for_b_ref):
    for_b_ref[:HALF] = w_ref[:HALF]
    for_a_ref[:HALF] = w_ref[HALF:]
    for i in range(HALF // 128):
        at = HALF + i * ROWS
        for_a_ref[at : at + ROWS] = rows_ref[:, i * 128 : (i + 1) * 128]
        for_b_ref[at : at + ROWS] = rows_ref[:, HALF + i * 128 : HALF + (i + 1) * 128]


def pack(rows, w, after):
    out = jax.ShapeDtypeStruct((HALF + HALF // 128 * ROWS, 128), rows.dtype)
    return pl.pallas_call(
        pack_kernel,
        out_shape=[out, out],
        in_specs=[VM, VM, ANY],
        out_specs=[VM] * 2,
        compiler_params=PARAMS,
        cost_estimate=cost(0, 4 * (rows.size + w.size)),
    )(rows, w, after)


def weights_kernel(from_a_ref, from_b_ref, piece_ref, q_ref, out_ref):
    out_ref[:HALF] = from_b_ref[:HALF]
    out_ref[HALF:] = from_a_ref[:HALF]


def weights(from_a, from_b, *after):
    return pl.pallas_call(
        weights_kernel,
        out_shape=jax.ShapeDtypeStruct((DEPTH, 128), from_a.dtype),
        in_specs=[VM, VM, ANY, ANY],
        out_specs=VM,
        compiler_params=PARAMS,
        cost_estimate=cost(0, 4 * DEPTH * 128),
    )(from_a, from_b, *after)


def project_kernel(
    where_ref, rows, own, other, from_a, from_b, came_other, local_ref, to_a_ref, to_b_ref
):
    first = where_ref[0] == 0

    def product(at, far, near):
        acc = None
        for k in range(0, HALF, 512):
            blocks = [HALF + (k // 128 + i) * ROWS for i in range(4)]
            x = jnp.concatenate([far[b : b + ROWS] for b in blocks], axis=1)
            x = jnp.concatenate([rows[:, at + k : at + k + 512], x], axis=0)
            w = jnp.concatenate(
                [
                    own[at + k : at + k + 512],
                    other[at + k : at + k + 512],
                    near[k : k + 512],
                    came_other[at + k : at + k + 512],
                ],
                axis=1,
            )
            got = jnp.dot(x, w, preferred_element_type=jnp.float32)
            acc = got if acc is None else acc + got
        a, b, c, d = (acc[:, i * 128 : (i + 1) * 128] for i in range(4))
        return jnp.concatenate(
            [
                jnp.where(first, a, b),
                jnp.where(first, b, a),
                jnp.where(first, c, d),
                jnp.where(first, d, c),
            ],
            axis=1,
        )

    one = product(0, from_a, from_b)
    two = product(HALF, from_b, from_a)
    local_ref[:, :256] = one[:ROWS, :256] + two[:ROWS, :256]
    local_ref[:, 256:512] = two[:ROWS, 256:]
    local_ref[:, 512:] = one[:ROWS, 256:]
    to_a_ref[...] = one[ROWS:].astype(jnp.bfloat16)
    to_b_ref[...] = two[ROWS:].astype(jnp.bfloat16)


def project(where, *arrays):
    back = jax.ShapeDtypeStruct((ROWS, 512), jnp.bfloat16)
    return pl.pallas_call(
        project_kernel,
        out_shape=[jax.ShapeDtypeStruct((ROWS, 768), jnp.float32), back, back],
        in_specs=[SM] + [VM] * 6,
        out_specs=[VM] * 3,
        compiler_params=PARAMS,
        cost_estimate=cost(4 * 2 * ROWS * HALF * 512, 7000000),
    )(where, *arrays)


def finish_kernel(where_ref, local_ref, got_a, got_b, gain_ref, cos_ref, sin_ref, out_ref, piece_ref):
    y = where_ref[1]
    even = (y & 1) == 0
    a = got_a[:, :256].astype(jnp.float32) + local_ref[:, 256:512]
    b = got_b[:, :256].astype(jnp.float32) + local_ref[:, 512:]
    piece_ref[0] = local_ref[:, :256]
    piece_ref[1] = jnp.where(even, a, b)
    piece_ref[2] = got_a[:, 256:].astype(jnp.float32) + got_b[:, 256:].astype(jnp.float32)
    piece_ref[3] = jnp.where(even, b, a)
    a, b, c, d = (piece_ref[(j - y) & 3] for j in range(4))
    keys = jnp.concatenate([a, b], axis=1)
    meansq = jnp.mean(keys * keys, axis=-1, keepdims=True)
    keys = keys * lax.rsqrt(meansq + 1e-06) * gain_ref[...]
    cosine, sine = cos_ref[...], sin_ref[...]
    for h in range(HEADS_KV):
        k = keys[:, h * HEAD : (h + 1) * HEAD]
        out_ref[:, h * HEAD : (h + 1) * HEAD] = (
            k * cosine + pltpu.roll(k, 64, 1) * sine
        ).astype(jnp.bfloat16)
    out_ref[:, 512:768] = c.astype(jnp.bfloat16)
    out_ref[:, 768:1024] = d.astype(jnp.bfloat16)


def finish(where, here, got_a, got_b, gain, cosine, sine):
    return pl.pallas_call(
        finish_kernel,
        out_shape=jax.ShapeDtypeStruct((ROWS, 1024), jnp.bfloat16),
        in_specs=[SM] + [VM] * 6,
        out_specs=VM,
        scratch_shapes=[pltpu.VMEM((4, ROWS, 256), jnp.float32)],
        compiler_params=PARAMS,
        cost_estimate=cost(64 * 512 * 10, 600000),
    )(where, here, got_a, got_b, gain, cosine, sine)


def queries(q_ref, g):
    first = g * GROUP
    return jnp.concatenate(
        [q_ref[:, (first + j) * HEAD : (first + j + 1) * HEAD] for j in range(GROUP)], axis=0
    )


def scores(q, k):
    return lax.dot_general(
        q, k, (((1,), (1,)), ((), ())), preferred_element_type=jnp.float32
    ) * SCALE


def merge_kernel(*refs):
    parts, out_ref = refs[:4], refs[-1]
    a, b, c, d = (p[...].astype(jnp.float32) for p in parts)
    out_ref[...] = (a + b + c + d).astype(jnp.bfloat16)


def merge(parts):
    return pl.pallas_call(
        merge_kernel,
        out_shape=jax.ShapeDtypeStruct(parts[0].shape, parts[0].dtype),
        in_specs=[VM] * 4,
        out_specs=VM,
        compiler_params=PARAMS,
        cost_estimate=cost(0, 10 * parts[0].size),
    )(*parts)


def prefix_kernel(n, q_ref, q2_ref, *refs):
    blocks, (high_ref, total_ref, sum_ref, send_ref) = refs[:n], refs[-4:]
    lane = lax.broadcasted_iota(jnp.int32, (ROWS, HEAD), 1)
    logs = jnp.zeros((ROWS, HEAD), jnp.float32)

    def attend(q, g):
        high = total = acc = None
        for block in blocks:
            s = scores(q, block[:, g * HEAD : (g + 1) * HEAD])
            v = block[:, KEY_WIDTH + g * HEAD : KEY_WIDTH + (g + 1) * HEAD]
            top = jnp.max(s, axis=-1, keepdims=True)
            new = top if high is None else jnp.maximum(high, top)
            p = jnp.exp2(s - new)
            part = jnp.sum(p, axis=-1, keepdims=True)
            pv = jnp.dot(p.astype(jnp.bfloat16), v, preferred_element_type=jnp.float32)
            if high is None:
                total, acc = part, pv
            else:
                factor = jnp.exp2(high - new)
                total, acc = total * factor + part, acc * factor + pv
            high = new
        return high, total, acc

    for g in range(HEADS_KV):
        high, total, acc = attend(queries(q2_ref, g), g)
        acc = (acc * (1.0 / total)).astype(jnp.bfloat16)
        log = high + jnp.log2(total)
        for j in range(GROUP):
            h = g * GROUP + j
            send_ref[:, h * HEAD : (h + 1) * HEAD] = acc[j * ROWS : (j + 1) * ROWS]
            logs = jnp.where(lane == h, log[j * ROWS : (j + 1) * ROWS], logs)
        high_ref[g], total_ref[g], sum_ref[g] = attend(queries(q_ref, g), g)
    for part in range(3):
        at = (20 + part) * HEAD
        piece = logs.astype(jnp.bfloat16)
        send_ref[:, at : at + HEAD] = piece
        logs = logs - piece.astype(jnp.float32)


def prefix_attend(q, q2, blocks, after):
    n = len(blocks)
    m = ROWS * GROUP
    keys = 2 * sum(b.shape[0] for b in blocks)
    return pl.pallas_call(
        functools.partial(prefix_kernel, n),
        out_shape=[
            jax.ShapeDtypeStruct((HEADS_KV, m, 1), jnp.float32),
            jax.ShapeDtypeStruct((HEADS_KV, m, 1), jnp.float32),
            jax.ShapeDtypeStruct((HEADS_KV, m, HEAD), jnp.float32),
            jax.ShapeDtypeStruct((ROWS, 23 * HEAD), jnp.bfloat16),
        ],
        in_specs=[VM] * (n + 2) + [ANY] * len(after),
        out_specs=[VM] * 4,
        compiler_params=PARAMS,
        cost_estimate=cost(4 * 1280 * keys * 128, keys * 2048 + 2000000, 1280 * keys),
    )(q, q2, *blocks, *after)


def last_kernel(
    where_ref, q_ref, t0, t1, t2, t3, own_ref, high_ref, total_ref, sum_ref, got_ref, out_ref, above_ref
):
    x, parent = where_ref[2], where_ref[3]
    child = parent >= 0
    d = (parent - x) & 3
    row = lax.broadcasted_iota(jnp.int32, (ROWS, 2 * ROWS), 0)
    col = lax.broadcasted_iota(jnp.int32, (ROWS, 2 * ROWS), 1)
    use = (jnp.where(child, 1, 0) * jnp.where(col < ROWS, 1, 0)) + jnp.where(
        (col >= ROWS) & (col - ROWS <= row), 1, 0
    )
    use = jnp.concatenate([use] * GROUP, axis=0) > 0

    for k, t in enumerate((t0, t1, t2, t3)):

        @pl.when(d == k)
        def _(t=t):
            above_ref[...] = t[...]

    logs = [got_ref[:, (20 + i) * HEAD : (21 + i) * HEAD].astype(jnp.float32) for i in range(3)]
    logs = logs[0] + logs[1] + logs[2]
    for g in range(HEADS_KV):
        q = queries(q_ref, g)
        lo, hi = g * HEAD, KEY_WIDTH + g * HEAD
        k = jnp.concatenate([above_ref[:, lo : lo + HEAD], own_ref[:, lo : lo + HEAD]], axis=0)
        v = jnp.concatenate([above_ref[:, hi : hi + HEAD], own_ref[:, hi : hi + HEAD]], axis=0)
        s = jnp.where(use, scores(q, k), NEG)
        heads = range(g * GROUP, (g + 1) * GROUP)
        high = high_ref[g]
        log = jnp.concatenate([logs[:, h : h + 1] for h in heads], axis=0)
        result = jnp.concatenate([got_ref[:, h * HEAD : (h + 1) * HEAD] for h in heads], axis=0)
        new = jnp.maximum(jnp.maximum(high, log), jnp.max(s, axis=-1, keepdims=True))
        p = jnp.exp2(s - new)
        factor, factor2 = jnp.exp2(high - new), jnp.exp2(log - new)
        total = total_ref[g] * factor + factor2 + jnp.sum(p, axis=-1, keepdims=True)
        acc = sum_ref[g] * factor + result.astype(jnp.float32) * factor2
        acc = acc + jnp.dot(p.astype(jnp.bfloat16), v, preferred_element_type=jnp.float32)
        acc = (acc * (1.0 / total)).astype(jnp.bfloat16)
        for j in range(GROUP):
            lo = (g * GROUP + j) * HEAD
            out_ref[:, lo : lo + HEAD] = acc[j * ROWS : (j + 1) * ROWS]


def last_attend(where, q, trunks, own, state, got):
    return pl.pallas_call(
        last_kernel,
        out_shape=jax.ShapeDtypeStruct((ROWS, HEADS_KV * GROUP * HEAD), jnp.bfloat16),
        in_specs=[SM] + [VM] * 10,
        out_specs=VM,
        scratch_shapes=[pltpu.VMEM((ROWS, 2 * KEY_WIDTH), jnp.bfloat16)],
        compiler_params=PARAMS,
        cost_estimate=cost(4 * 1280 * 128 * 128, 3000000, 1280 * 128),
    )(where, q, *trunks, own, *state, got)


def local(x_branch, w_kv, k_gain, q_branch, prefix_kv, tree_parent):
    y, core = lax.axis_index(Y), lax.axis_index("core")
    parent = tree_parent[0, 0]
    where = jnp.stack([core, y, lax.axis_index("x"), parent]).astype(jnp.int32)

    piece = prefix_kv[0]
    facing = along_y(piece, [(i, (i + 4) % 8) for i in range(8)])

    rows = x_branch[0]
    for_a, for_b = pack(rows, w_kv, facing)
    from_a = along_y(for_a, NEXT_A)
    from_b = along_y(for_b, NEXT_B)
    w_other = swap(w_kv)

    q = q_branch[0]
    q2 = ring_x(q, X_NEXT_A)

    piece = join([piece, facing])
    for bit in (4, 2):
        piece = join([piece, along_z(piece, bit)])
    far = along_z(piece, 1)
    came_other = swap(weights(from_a, from_b, piece, q2))
    here, to_a, to_b = project(where, rows, w_kv, w_other, from_a, from_b, came_other)
    got_a = along_y(to_a, NEXT_A)
    got_b = along_y(to_b, NEXT_B)
    piece = join([piece, far], [got_a, got_b])
    beside = ring_x(piece, X_NEXT_B)

    index = jnp.arange(64, dtype=jnp.float32)
    inverse = jnp.exp(-jnp.log(jnp.float32(500000.0)) * 2.0 * index / HEAD)
    inside = jnp.arange(ROWS, dtype=jnp.int32)
    positions = PREFIX + inside + ROWS * (parent >= 0).astype(jnp.int32)
    angle = positions.astype(jnp.float32)[:, None] * inverse[None, :]
    cosine, sine = jnp.cos(angle), jnp.sin(angle)
    cosine = jnp.concatenate([cosine, cosine], axis=1)
    sine = jnp.concatenate([-sine, sine], axis=1)
    own = finish(where, here, got_a, got_b, k_gain[None, :], cosine, sine)

    root = (lax.axis_index("yh") == 0) & (lax.axis_index("z") == 0)
    parts = [jnp.where(root, own, jnp.zeros_like(own))]
    parts += [along_yh_z(own, [(0, 0) + far]) for far in ((1, 0), (0, 2), (0, 6))]
    have = merge(parts)
    trunk = have
    for targets in (
        ((0, 4), (1, 2), (1, 6), (1, 4)),
        ((0, 1), (0, 3), (0, 5), (1, 1)),
        ((0, 7), (1, 3), (1, 5), (1, 7)),
    ):
        holders = ((0, 0), (0, 2), (0, 6), (1, 0))
        trunk = trunk + along_yh_z(have, [a + b for a, b in zip(holders, targets)])

    *state, partial = prefix_attend(q, q2, [piece, beside], [have])
    got = ring_x(partial, X_NEXT_A)
    opposite = along_x(trunk, 2)
    trunks = [trunk, along_x(trunk, -1), opposite, along_x(trunk, 1)]
    return last_attend(where, q, trunks, own, state, got)[None]


def solution(mesh):
    parts = jax.sharding.Mesh(mesh.devices.reshape(SIZES), PARTS)
    tokens = P(NARROW, WIDE, None)
    placed = (tokens, P(None, NARROW), P(), tokens, tokens, P(NARROW, WIDE))
    return jax.shard_map(local, mesh=parts, in_specs=placed, out_specs=tokens, check_vma=False)
```

```python
import functools
import math

import jax
import jax.numpy as jnp
from jax import lax
from jax.experimental import pallas as pl
from jax.experimental.pallas import tpu as pltpu
from jax.sharding import PartitionSpec as P

HEAD = 128
HEADS_KV = 4
GROUP = 5
ROWS = 64
KEY_WIDTH = 512
PREFIX = 1024
SCALE = HEAD ** -0.5 * math.log2(math.e)
NEG = -1e30

PARTS = ("yh", "z", "x", "yl", "core")
SIZES = (2, 8, 4, 4, 2)
WIDE, NARROW = PARTS[:3], PARTS[3:]
Y = ("yh", "yl")


NEXT_A = [(i, i ^ 1) for i in range(8)]
NEXT_B = [(i, (i + (1 if i % 2 else -1)) % 8) for i in range(8)]


X_NEXT_A = [(i, i ^ 1) for i in range(4)]
X_NEXT_B = [(i, 3 - i) for i in range(4)]


def ring_x(value, pairs):
    return lax.ppermute(value, "x", pairs)


def along_x(value, s):
    return lax.ppermute(value, "x", [(i, (i + s) % 4) for i in range(4)])


def along_y(value, pairs):
    return lax.ppermute(value, Y, pairs)


def along_z(value, bit):
    return lax.ppermute(value, "z", [(i, i ^ bit) for i in range(8)])


def swap(value):
    return lax.ppermute(value, "core", [(0, 1), (1, 0)])


def along_yh_z(value, pairs):
    return lax.ppermute(value, ("yh", "z"), [(a * 8 + b, c * 8 + d) for a, b, c, d in pairs])


VM = pl.BlockSpec(memory_space=pltpu.VMEM)
SM = pl.BlockSpec(memory_space=pltpu.SMEM)
PARAMS = pltpu.CompilerParams(vmem_limit_bytes=20 * 1024 * 1024)


def cost(flops, moved, trans=0):
    return pl.CostEstimate(flops=flops, bytes_accessed=moved, transcendentals=trans)


ANY = pl.BlockSpec(memory_space=pl.ANY)
DEPTH = 5120
HALF = DEPTH // 2


def join_kernel(n, *refs):
    parts, out_ref = refs[:n], refs[-1]
    at = 0
    for part in parts:
        out_ref[at : at + part.shape[0]] = part[...]
        at += part.shape[0]


def join(parts, after=()):
    n = len(parts)
    total = sum(p.shape[0] for p in parts)
    width = parts[0].shape[1]
    return pl.pallas_call(
        functools.partial(join_kernel, n),
        out_shape=jax.ShapeDtypeStruct((total, width), parts[0].dtype),
        in_specs=[VM] * n + [ANY] * len(after),
        out_specs=VM,
        compiler_params=PARAMS,
        cost_estimate=cost(0, 4 * total * width),
    )(*parts, *after)


def pack_kernel(rows_ref, w_ref, after_ref, for_a_ref, for_b_ref):
    for_b_ref[:HALF] = w_ref[:HALF]
    for_a_ref[:HALF] = w_ref[HALF:]
    for i in range(HALF // 128):
        at = HALF + i * ROWS
        for_a_ref[at : at + ROWS] = rows_ref[:, i * 128 : (i + 1) * 128]
        for_b_ref[at : at + ROWS] = rows_ref[:, HALF + i * 128 : HALF + (i + 1) * 128]


def pack(rows, w, after):
    out = jax.ShapeDtypeStruct((HALF + HALF // 128 * ROWS, 128), rows.dtype)
    return pl.pallas_call(
        pack_kernel,
        out_shape=[out, out],
        in_specs=[VM, VM, ANY],
        out_specs=[VM] * 2,
        compiler_params=PARAMS,
        cost_estimate=cost(0, 4 * (rows.size + w.size)),
    )(rows, w, after)


def weights_kernel(from_a_ref, from_b_ref, piece_ref, q_ref, out_ref):
    out_ref[:HALF] = from_b_ref[:HALF]
    out_ref[HALF:] = from_a_ref[:HALF]


def weights(from_a, from_b, *after):
    return pl.pallas_call(
        weights_kernel,
        out_shape=jax.ShapeDtypeStruct((DEPTH, 128), from_a.dtype),
        in_specs=[VM, VM, ANY, ANY],
        out_specs=VM,
        compiler_params=PARAMS,
        cost_estimate=cost(0, 4 * DEPTH * 128),
    )(from_a, from_b, *after)


def project_kernel(
    where_ref, rows, own, other, from_a, from_b, came_other, local_ref, to_a_ref, to_b_ref
):
    first = where_ref[0] == 0

    def product(at, far, near):
        acc = None
        for k in range(0, HALF, 512):
            blocks = [HALF + (k // 128 + i) * ROWS for i in range(4)]
            x = jnp.concatenate([far[b : b + ROWS] for b in blocks], axis=1)
            x = jnp.concatenate([rows[:, at + k : at + k + 512], x], axis=0)
            w = jnp.concatenate(
                [
                    own[at + k : at + k + 512],
                    other[at + k : at + k + 512],
                    near[k : k + 512],
                    came_other[at + k : at + k + 512],
                ],
                axis=1,
            )
            got = jnp.dot(x, w, preferred_element_type=jnp.float32)
            acc = got if acc is None else acc + got
        a, b, c, d = (acc[:, i * 128 : (i + 1) * 128] for i in range(4))
        return jnp.concatenate(
            [
                jnp.where(first, a, b),
                jnp.where(first, b, a),
                jnp.where(first, c, d),
                jnp.where(first, d, c),
            ],
            axis=1,
        )

    one = product(0, from_a, from_b)
    two = product(HALF, from_b, from_a)
    local_ref[:, :256] = one[:ROWS, :256] + two[:ROWS, :256]
    local_ref[:, 256:512] = two[:ROWS, 256:]
    local_ref[:, 512:] = one[:ROWS, 256:]
    to_a_ref[...] = one[ROWS:].astype(jnp.bfloat16)
    to_b_ref[...] = two[ROWS:].astype(jnp.bfloat16)


def project(where, *arrays):
    back = jax.ShapeDtypeStruct((ROWS, 512), jnp.bfloat16)
    return pl.pallas_call(
        project_kernel,
        out_shape=[jax.ShapeDtypeStruct((ROWS, 768), jnp.float32), back, back],
        in_specs=[SM] + [VM] * 6,
        out_specs=[VM] * 3,
        compiler_params=PARAMS,
        cost_estimate=cost(4 * 2 * ROWS * HALF * 512, 7000000),
    )(where, *arrays)


def finish_kernel(where_ref, local_ref, got_a, got_b, gain_ref, cos_ref, sin_ref, out_ref, piece_ref):
    y = where_ref[1]
    even = (y & 1) == 0
    a = got_a[:, :256].astype(jnp.float32) + local_ref[:, 256:512]
    b = got_b[:, :256].astype(jnp.float32) + local_ref[:, 512:]
    piece_ref[0] = local_ref[:, :256]
    piece_ref[1] = jnp.where(even, a, b)
    piece_ref[2] = got_a[:, 256:].astype(jnp.float32) + got_b[:, 256:].astype(jnp.float32)
    piece_ref[3] = jnp.where(even, b, a)
    a, b, c, d = (piece_ref[(j - y) & 3] for j in range(4))
    keys = jnp.concatenate([a, b], axis=1)
    meansq = jnp.mean(keys * keys, axis=-1, keepdims=True)
    keys = keys * lax.rsqrt(meansq + 1e-06) * gain_ref[...]
    cosine, sine = cos_ref[...], sin_ref[...]
    for h in range(HEADS_KV):
        k = keys[:, h * HEAD : (h + 1) * HEAD]
        out_ref[:, h * HEAD : (h + 1) * HEAD] = (
            k * cosine + pltpu.roll(k, 64, 1) * sine
        ).astype(jnp.bfloat16)
    out_ref[:, 512:768] = c.astype(jnp.bfloat16)
    out_ref[:, 768:1024] = d.astype(jnp.bfloat16)


def finish(where, here, got_a, got_b, gain, cosine, sine):
    return pl.pallas_call(
        finish_kernel,
        out_shape=jax.ShapeDtypeStruct((ROWS, 1024), jnp.bfloat16),
        in_specs=[SM] + [VM] * 6,
        out_specs=VM,
        scratch_shapes=[pltpu.VMEM((4, ROWS, 256), jnp.float32)],
        compiler_params=PARAMS,
        cost_estimate=cost(64 * 512 * 10, 600000),
    )(where, here, got_a, got_b, gain, cosine, sine)


def queries(q_ref, g):
    first = g * GROUP
    return jnp.concatenate(
        [q_ref[:, (first + j) * HEAD : (first + j + 1) * HEAD] for j in range(GROUP)], axis=0
    )


def scores(q, k):
    return lax.dot_general(
        q, k, (((1,), (1,)), ((), ())), preferred_element_type=jnp.float32
    ) * SCALE


def merge_kernel(*refs):
    parts, out_ref = refs[:4], refs[-1]
    a, b, c, d = (p[...].astype(jnp.float32) for p in parts)
    out_ref[...] = (a + b + c + d).astype(jnp.bfloat16)


def merge(parts):
    return pl.pallas_call(
        merge_kernel,
        out_shape=jax.ShapeDtypeStruct(parts[0].shape, parts[0].dtype),
        in_specs=[VM] * 4,
        out_specs=VM,
        compiler_params=PARAMS,
        cost_estimate=cost(0, 10 * parts[0].size),
    )(*parts)


def attend_prefix(q, blocks, g):
    high = total = acc = None
    for block in blocks:
        s = scores(q, block[:, g * HEAD : (g + 1) * HEAD])
        v = block[:, KEY_WIDTH + g * HEAD : KEY_WIDTH + (g + 1) * HEAD]
        top = jnp.max(s, axis=-1, keepdims=True)
        new = top if high is None else jnp.maximum(high, top)
        p = jnp.exp2(s - new)
        part = jnp.sum(p, axis=-1, keepdims=True)
        pv = jnp.dot(p.astype(jnp.bfloat16), v, preferred_element_type=jnp.float32)
        if high is None:
            total, acc = part, pv
        else:
            factor = jnp.exp2(high - new)
            total, acc = total * factor + part, acc * factor + pv
        high = new
    return high, total, acc


def partner_kernel(q_ref, one_ref, two_ref, after_ref, send_ref):
    lane = lax.broadcasted_iota(jnp.int32, (ROWS, HEAD), 1)
    logs = jnp.zeros((ROWS, HEAD), jnp.float32)
    for g in range(HEADS_KV):
        high, total, acc = attend_prefix(queries(q_ref, g), [one_ref, two_ref], g)
        acc = (acc * (1.0 / total)).astype(jnp.bfloat16)
        log = high + jnp.log2(total)
        for j in range(GROUP):
            h = g * GROUP + j
            send_ref[:, h * HEAD : (h + 1) * HEAD] = acc[j * ROWS : (j + 1) * ROWS]
            logs = jnp.where(lane == h, log[j * ROWS : (j + 1) * ROWS], logs)
    for part in range(3):
        at = (20 + part) * HEAD
        piece = logs.astype(jnp.bfloat16)
        send_ref[:, at : at + HEAD] = piece
        logs = logs - piece.astype(jnp.float32)


def own_kernel(q_ref, one_ref, two_ref, after_ref, high_ref, total_ref, sum_ref):
    for g in range(HEADS_KV):
        high_ref[g], total_ref[g], sum_ref[g] = attend_prefix(
            queries(q_ref, g), [one_ref, two_ref], g
        )


def prefix_attend(kernel, out_shape, q, one, two, after):
    keys = one.shape[0] + two.shape[0]
    return pl.pallas_call(
        kernel,
        out_shape=out_shape,
        in_specs=[VM] * 3 + [ANY],
        out_specs=[VM] * len(out_shape),
        compiler_params=PARAMS,
        cost_estimate=cost(4 * 1280 * keys * 128, keys * 2048 + 1000000, 1280 * keys),
    )(q, one, two, after)


PARTIAL = [jax.ShapeDtypeStruct((ROWS, 23 * HEAD), jnp.bfloat16)]
STATE = [
    jax.ShapeDtypeStruct((HEADS_KV, ROWS * GROUP, 1), jnp.float32),
    jax.ShapeDtypeStruct((HEADS_KV, ROWS * GROUP, 1), jnp.float32),
    jax.ShapeDtypeStruct((HEADS_KV, ROWS * GROUP, HEAD), jnp.float32),
]


def last_kernel(
    where_ref, q_ref, t0, t1, t2, t3, own_ref, high_ref, total_ref, sum_ref, got_ref, out_ref, above_ref
):
    x, parent = where_ref[2], where_ref[3]
    child = parent >= 0
    d = (parent - x) & 3
    row = lax.broadcasted_iota(jnp.int32, (ROWS, 2 * ROWS), 0)
    col = lax.broadcasted_iota(jnp.int32, (ROWS, 2 * ROWS), 1)
    use = (jnp.where(child, 1, 0) * jnp.where(col < ROWS, 1, 0)) + jnp.where(
        (col >= ROWS) & (col - ROWS <= row), 1, 0
    )
    use = jnp.concatenate([use] * GROUP, axis=0) > 0

    for k, t in enumerate((t0, t1, t2, t3)):

        @pl.when(d == k)
        def _(t=t):
            above_ref[...] = t[...]

    logs = [got_ref[:, (20 + i) * HEAD : (21 + i) * HEAD].astype(jnp.float32) for i in range(3)]
    logs = logs[0] + logs[1] + logs[2]
    for g in range(HEADS_KV):
        q = queries(q_ref, g)
        lo, hi = g * HEAD, KEY_WIDTH + g * HEAD
        k = jnp.concatenate([above_ref[:, lo : lo + HEAD], own_ref[:, lo : lo + HEAD]], axis=0)
        v = jnp.concatenate([above_ref[:, hi : hi + HEAD], own_ref[:, hi : hi + HEAD]], axis=0)
        s = jnp.where(use, scores(q, k), NEG)
        heads = range(g * GROUP, (g + 1) * GROUP)
        high = high_ref[g]
        log = jnp.concatenate([logs[:, h : h + 1] for h in heads], axis=0)
        result = jnp.concatenate([got_ref[:, h * HEAD : (h + 1) * HEAD] for h in heads], axis=0)
        new = jnp.maximum(jnp.maximum(high, log), jnp.max(s, axis=-1, keepdims=True))
        p = jnp.exp2(s - new)
        factor, factor2 = jnp.exp2(high - new), jnp.exp2(log - new)
        total = total_ref[g] * factor + factor2 + jnp.sum(p, axis=-1, keepdims=True)
        acc = sum_ref[g] * factor + result.astype(jnp.float32) * factor2
        acc = acc + jnp.dot(p.astype(jnp.bfloat16), v, preferred_element_type=jnp.float32)
        acc = (acc * (1.0 / total)).astype(jnp.bfloat16)
        for j in range(GROUP):
            lo = (g * GROUP + j) * HEAD
            out_ref[:, lo : lo + HEAD] = acc[j * ROWS : (j + 1) * ROWS]


def last_attend(where, q, trunks, own, state, got):
    return pl.pallas_call(
        last_kernel,
        out_shape=jax.ShapeDtypeStruct((ROWS, HEADS_KV * GROUP * HEAD), jnp.bfloat16),
        in_specs=[SM] + [VM] * 10,
        out_specs=VM,
        scratch_shapes=[pltpu.VMEM((ROWS, 2 * KEY_WIDTH), jnp.bfloat16)],
        compiler_params=PARAMS,
        cost_estimate=cost(4 * 1280 * 128 * 128, 3000000, 1280 * 128),
    )(where, q, *trunks, own, *state, got)


def local(x_branch, w_kv, k_gain, q_branch, prefix_kv, tree_parent):
    y, core = lax.axis_index(Y), lax.axis_index("core")
    parent = tree_parent[0, 0]
    where = jnp.stack([core, y, lax.axis_index("x"), parent]).astype(jnp.int32)

    piece = prefix_kv[0]
    facing = along_y(piece, [(i, (i + 4) % 8) for i in range(8)])

    rows = x_branch[0]
    for_a, for_b = pack(rows, w_kv, facing)
    from_a = along_y(for_a, NEXT_A)
    from_b = along_y(for_b, NEXT_B)
    w_other = swap(w_kv)

    q = q_branch[0]
    q2 = ring_x(q, X_NEXT_A)

    piece = join([piece, facing])
    for bit in (4, 2):
        piece = join([piece, along_z(piece, bit)])
    far = along_z(piece, 1)
    came_other = swap(weights(from_a, from_b, piece, q2))
    here, to_a, to_b = project(where, rows, w_kv, w_other, from_a, from_b, came_other)
    got_a = along_y(to_a, NEXT_A)
    got_b = along_y(to_b, NEXT_B)
    piece = join([piece, far], [got_a, got_b])
    beside = ring_x(piece, X_NEXT_B)

    index = jnp.arange(64, dtype=jnp.float32)
    inverse = jnp.exp(-jnp.log(jnp.float32(500000.0)) * 2.0 * index / HEAD)
    inside = jnp.arange(ROWS, dtype=jnp.int32)
    positions = PREFIX + inside + ROWS * (parent >= 0).astype(jnp.int32)
    angle = positions.astype(jnp.float32)[:, None] * inverse[None, :]
    cosine, sine = jnp.cos(angle), jnp.sin(angle)
    cosine = jnp.concatenate([cosine, cosine], axis=1)
    sine = jnp.concatenate([-sine, sine], axis=1)
    own = finish(where, here, got_a, got_b, k_gain[None, :], cosine, sine)

    root = (lax.axis_index("yh") == 0) & (lax.axis_index("z") == 0)
    parts = [jnp.where(root, own, jnp.zeros_like(own))]
    parts += [along_yh_z(own, [(0, 0) + far]) for far in ((1, 0), (0, 2), (0, 6))]
    have = merge(parts)
    trunk = have
    for targets in (
        ((0, 4), (1, 2), (1, 6), (1, 4)),
        ((0, 1), (0, 3), (0, 5), (1, 1)),
        ((0, 7), (1, 3), (1, 5), (1, 7)),
    ):
        holders = ((0, 0), (0, 2), (0, 6), (1, 0))
        trunk = trunk + along_yh_z(have, [a + b for a, b in zip(holders, targets)])

    (partial,) = prefix_attend(partner_kernel, PARTIAL, q2, piece, beside, have)
    state = prefix_attend(own_kernel, STATE, q, piece, beside, trunk)
    got = ring_x(partial, X_NEXT_A)
    opposite = along_x(trunk, 2)
    trunks = [trunk, along_x(trunk, -1), opposite, along_x(trunk, 1)]
    return last_attend(where, q, trunks, own, state, got)[None]


def solution(mesh):
    parts = jax.sharding.Mesh(mesh.devices.reshape(SIZES), PARTS)
    tokens = P(NARROW, WIDE, None)
    placed = (tokens, P(None, NARROW), P(), tokens, tokens, P(NARROW, WIDE))
    return jax.shard_map(local, mesh=parts, in_specs=placed, out_specs=tokens, check_vma=False)
```
